32 devices in a mesh: rows: 8 (over z, x), cent: 4 (over y, core).
Axes of the slice: x: 2, y: 2, z: 4, core: 2. Of those that a mesh axis runs over, the one named last changes fastest.
Arguments:
- emb_values: bfloat16 [4096, 1024], P(('cent', 'rows')), may hold values from -6 to 6
- emb_scales: bfloat16 [4096, 8], P(('cent', 'rows')), may hold values from 0.125 to 8, as said below
- coarse_ids: int32 [4, 1024], P(None, 'rows'), may hold values from 0 to 8191, as said below
- centroids: bfloat16 [8192, 1024], P('cent'), may hold values from -6 to 6
- codes_one: int32 [16, 4096], P('rows', 'cent'), may hold values from 0 to 255
- codes_two: int32 [16, 4096], P('rows', 'cent'), may hold values from 0 to 255
- codebook_init: float32 [16, 256, 64], P('rows'), may hold values from -6 to 6
Outputs:
- coarse_gap: float32 [4096], P(('cent', 'rows'))
- codebook_one: float32 [16, 256, 64], P('rows')
- codebook_two: float32 [16, 256, 64], P('rows')
- distortion: float32 [16, 4096], P('rows', 'cent')
The draws below stay inside these ranges and needn't reach their ends.
Inputs may be any that keep to these rules, and one draw needn't show every extreme that they name: `coarse_ids`: in each aligned block of 128 rows of the flattened ids (the rows of one device), at most 64 ids fall in any one aligned range of 2048 centroids, and exactly 64 fall in some range. `emb_scales`: every scale is a power of two.
All inputs are finite; a program needn't handle non-finite values.
Results may differ from the reference program's by a relative error of at most 0.0003.
Values may be sent and summed in bfloat16 or wider, within the bound.
A program may use at most 64 MiB of HBM per device.

```python
import math
import jax
import jax.numpy as jnp
import numpy as np
from jax import lax

D = 1024
BLOCK = 128
M = 16
K = 256
CENT_DEV = 2048
ROWS_DEV = 128
ROWS = 4096
CENTROIDS = 8192
BLOCKS = 8
SUB = 64


def draw_emb_scales(key, part):
    low_power, high_power = (-2, 3)
    powers = jax.random.randint(jax.random.fold_in(key, 11), (ROWS, BLOCKS), low_power, high_power)
    return jnp.exp2(powers.astype(jnp.float32)).astype(jnp.bfloat16)


def draw_coarse_ids(key, part):
    groups = ROWS // ROWS_DEV
    owners = CENTROIDS // CENT_DEV
    limit = max(2, 2 * ROWS_DEV // owners)

    def one_group(group_key):
        key_heavy, key_slots, key_order, key_local = jax.random.split(group_key, 4)
        heavy = jax.random.randint(key_heavy, (), 0, owners).astype(jnp.int32)
        slots = jax.random.permutation(key_slots, (owners - 1) * limit)[:ROWS_DEV - limit].astype(jnp.int32)
        others = (heavy + 1 + slots // limit) % owners
        owner = jnp.concatenate([jnp.zeros((limit,), jnp.int32) + heavy, others])
        owner = jax.random.permutation(key_order, owner)
        local = jax.random.randint(key_local, (ROWS_DEV,), 0, CENT_DEV).astype(jnp.int32)
        return owner * CENT_DEV + local
    group_keys = jax.random.split(jax.random.fold_in(key, 7), groups)
    drawn = jax.vmap(one_group)(group_keys)
    return drawn.reshape(owners, groups // owners * ROWS_DEV).astype(jnp.int32)


def place_ends(values, rng, least, largest):
    longest = values.shape.index(max(values.shape))
    spots = []
    for shift in (0, 1):
        where = [jax.random.randint(jax.random.fold_in(rng, axis), (), 0, length) for axis, length in enumerate(values.shape)]
        where[longest] = (where[longest] + shift) % values.shape[longest]
        spots.append(tuple(where))
    return values.at[spots[0]].set(least).at[spots[1]].set(largest)


def block_levels(rng, extent, cuts, least, largest):
    def one(axis_at, shards_of):
        draws = jax.random.uniform(jax.random.fold_in(jax.random.fold_in(rng, 6), axis_at), (shards_of,), jnp.float32, least / len(cuts), largest / len(cuts))
        return jnp.repeat(jnp.exp(draws), extent[axis_at] // shards_of).reshape((-1,) + (1,) * (len(extent) - axis_at - 1))

    factor_of = one(*cuts[0])
    for cut in cuts[1:]:
        factor_of = factor_of * one(*cut)
    return factor_of


def rank_table(count, lean):
    loads = [(1 << 20) // math.isqrt(rank ** lean) + 1 for rank in range(1, count + 1)]
    deviation = 1 + sum(loads) // (1 << 30)
    return np.cumsum(np.array([max(1, weight // deviation) for weight in loads]))


def ranked_ids(key, extent, number_of, skew):
    listing = rank_table(number_of, skew)
    lot = jax.random.randint(jax.random.fold_in(key, 1), extent, 0, int(listing[number_of - 1]))
    rank = jnp.searchsorted(jnp.asarray(listing, jnp.int32), lot, side="right")
    return jax.random.permutation(jax.random.fold_in(key, 2), number_of)[rank].astype(jnp.int32)


def noise(stream_key, shape, scale, most, shards=(), held_as=jnp.bfloat16):
    entries = scale * jax.random.normal(stream_key, shape, jnp.float32)
    if shards:
        entries = entries * block_levels(stream_key, shape, shards, -0.22, 0.18)
    return jnp.clip(entries, -most, most).astype(held_as)


def setup_inputs(seed: int = 0) -> dict:
    streams_of = jax.random.split(jax.random.key(seed), 8)
    return {
        "emb_values": noise(streams_of[0], (ROWS, D), 1.0, 6.0, ((0, 32),)),
        "emb_scales": draw_emb_scales(jax.random.fold_in(streams_of[7], 71), 0),
        "coarse_ids": draw_coarse_ids(jax.random.fold_in(streams_of[7], 71), 0),
        "centroids": noise(streams_of[3], (CENTROIDS, D), 1.0, 6.0, ((0, 4),)),
        "codes_one": place_ends(ranked_ids(streams_of[4], (M, ROWS), K, 2), jax.random.fold_in(streams_of[4], 3), 0, K - 1).astype(jnp.int32),
        "codes_two": place_ends(ranked_ids(streams_of[5], (M, ROWS), K, 2), jax.random.fold_in(streams_of[5], 3), 0, K - 1).astype(jnp.int32),
        "codebook_init": noise(streams_of[6], (M, K, SUB), 1.0, 6.0, ((0, 8),), jnp.float32),
    }


prior_weight = 8.0


def reference(emb_values, emb_scales, coarse_ids, centroids, codes_one, codes_two, codebook_init):
    dequantized = emb_values.astype(jnp.float32) * jnp.repeat(emb_scales.astype(jnp.float32), BLOCK, axis=1)
    quantized = dequantized.astype(jnp.bfloat16)
    cent_squares = jnp.sum(jnp.square(centroids.astype(jnp.float32)), axis=1)
    block_rows = min(512, ROWS)

    def nearest_block(row_batch):
        row_squares = jnp.sum(jnp.square(row_batch.astype(jnp.float32)), axis=1)
        cross_terms = lax.dot_general(row_batch, centroids, (((1,), (1,)), ((), ())), preferred_element_type=jnp.float32)
        distances = row_squares[:, None] - 2.0 * cross_terms + cent_squares[None, :]
        return jnp.min(distances, axis=1)

    group_best = lax.map(nearest_block, quantized.reshape(ROWS // block_rows, block_rows, D)).reshape(ROWS)
    coarse_gap = group_best / D
    flat_ids = coarse_ids.reshape(ROWS).astype(jnp.int32)
    fetched = jnp.take(centroids, flat_ids, axis=0).astype(jnp.float32)
    residual = dequantized - fetched
    stacked = residual.T.reshape(M, SUB, ROWS)

    def per_space(space_items):
        space_rows, first_codes, second_codes, init_book = space_items
        codeword_ids = jnp.arange(K, dtype=jnp.int32)
        one_first = (first_codes[None, :] == codeword_ids[:, None]).astype(jnp.float32)
        totals_one = jnp.dot(one_first, space_rows.T, precision=lax.Precision.HIGHEST)
        counts_one = jnp.sum(one_first, axis=1)
        book_one = (totals_one + prior_weight * init_book) / (counts_one + prior_weight)[:, None]
        one_second = (second_codes[None, :] == codeword_ids[:, None]).astype(jnp.float32)
        totals_two = jnp.dot(one_second, space_rows.T, precision=lax.Precision.HIGHEST)
        counts_two = jnp.sum(one_second, axis=1)
        book_two = (totals_two + prior_weight * book_one) / (counts_two + prior_weight)[:, None]
        rebuilt = jnp.dot(book_two.T, one_second, precision=lax.Precision.HIGHEST)
        difference = space_rows - rebuilt
        return book_one, book_two, jnp.sum(difference * difference, axis=0) / SUB

    book_one, book_two, distortion = lax.map(per_space, (stacked, codes_one, codes_two, codebook_init))
    return coarse_gap, book_one, book_two, distortion
```

```python
import functools

import jax
import jax.numpy as jnp
from jax import lax
from jax.experimental import pallas as pl
from jax.experimental.pallas import tpu as pltpu
from jax.sharding import PartitionSpec as P

prior_weight = 8.0
MESH = pl.DeviceIdType.MESH
F32, BF16 = jnp.float32, jnp.bfloat16


def dot(a, b, ca, cb):
    return lax.dot_general(a, b, (((ca,), (cb,)), ((), ())), preferred_element_type=F32)


def split(x):
    hi = x.astype(BF16)
    return hi, (x - hi.astype(F32)).astype(BF16)


def kernel(
    C, R,
    val_ref, scale_ref, ids_ref, cent_hbm, one_ref, two_ref, init_ref,
    gap_ref, book1_ref, book2_ref, dist_ref,
    cent, qg, stage, deqc, ids_pad, ids_all, keys, hot, comp_send, comp_recv,
    csq, minbuf, minrecv, xt, oh, st, st_in, st_half, st_out,
    cent_sem, ids_s, ids_r, col_s, col_r, row_s, row_r, pair_s, pair_r,
    comp_s, comp_r, min_s, min_r, s1_s, s1_r, s2_s, s2_r, s3_s, s3_r,
):
    r, c = lax.axis_index("rows"), lax.axis_index("cent")
    N, D = val_ref.shape
    L = cent.shape[0]
    w = stage.shape[2]
    msub = one_ref.shape[0]
    sub = w // msub
    K = init_ref.shape[1]
    lim = comp_send.shape[2]
    Cp = ids_pad.shape[0]
    half = C // 2
    core = lax.rem(c, 2)
    partner = c + 1 - 2 * core
    chip = c // 2

    def at_cent(p):
        return (r, p)

    def at_rows(p):
        return (p, c)

    def remote(src, dst, s, rr, dev):
        return pltpu.make_async_remote_copy(
            src_ref=src, dst_ref=dst, send_sem=s, recv_sem=rr, device_id=dev, device_id_type=MESH
        )

    load = pltpu.make_async_copy(cent_hbm, cent, cent_sem)
    load.start()
    barrier = pltpu.get_barrier_semaphore()
    for d in range(1, C):
        pl.semaphore_signal(barrier, inc=1, device_id=at_cent(lax.rem(c + d, C)), device_id_type=MESH)
    for d in range(1, R):
        pl.semaphore_signal(barrier, inc=1, device_id=at_rows(lax.rem(r + d, R)), device_id_type=MESH)

    width = D // scale_ref.shape[1]
    scales = scale_ref[...].astype(F32)
    squares = jnp.zeros((N, 128), F32)
    for b in range(D // width):
        part = val_ref[:, b * width:(b + 1) * width].astype(F32) * scales[:, b:b + 1]
        part = part.astype(BF16)
        qg[c, :, b * width:(b + 1) * width] = part
        wide = part.astype(F32)
        for e in range(width // 128):
            squares = squares + jnp.square(wide[:, e * 128:(e + 1) * 128])
    for j in range(R):
        stage[j] = qg[c, :, j * w:(j + 1) * w]
    ids_pad[...] = jnp.full(ids_pad.shape, -1, jnp.int32)
    ids_pad[0:C] = ids_ref[...]
    ids_all[r] = ids_pad[...]
    deqc[r] = stage[r]

    pl.semaphore_wait(barrier, C - 1 + R - 1)

    sends = []

    def go(copy):
        copy.start()
        sends.append(copy)

    for d in range(1, R):
        p = lax.rem(r + d, R)
        go(remote(ids_pad, ids_all.at[r], ids_s.at[d], ids_r.at[d], at_rows(p)))
    for e in range(1, half):
        p = lax.rem(c + 2 * e, C)
        go(remote(qg.at[c], qg.at[c], row_s.at[e], row_r.at[e], at_cent(p)))
    go(remote(qg.at[c], qg.at[c], pair_s.at[0], pair_r.at[0], at_cent(partner)))
    for d in range(1, R):
        p = lax.rem(r + d, R)
        go(remote(stage.at[p], deqc.at[r], col_s.at[d], col_r.at[d], at_rows(p)))

    iota_k = lax.broadcasted_iota(jnp.int32, (K, one_ref.shape[1]), 0)
    for t, ref in enumerate((one_ref, two_ref)):
        for m in range(msub):
            oh[t, m] = jnp.where(ref[m:m + 1, :] == iota_k, 1.0, 0.0).astype(BF16)

    for d in range(1, R):
        p = lax.rem(r + R - d, R)
        remote(ids_pad, ids_all.at[p], ids_s.at[d], ids_r.at[d], at_rows(p)).wait_recv()
    ids = ids_all[...].reshape(R * Cp, N)
    before = jnp.where(
        lax.broadcasted_iota(jnp.int32, (N, N), 0) < lax.broadcasted_iota(jnp.int32, (N, N), 1), 1.0, 0.0
    ).astype(BF16)
    for p in range(C):
        mask = (ids >= p * L) & (ids < (p + 1) * L)
        rank = dot(jnp.where(mask, 1.0, 0.0).astype(BF16), before, 1, 0)
        keys[p] = jnp.where(mask, rank, -1.0)

    load.wait()
    iota_slot = lax.broadcasted_iota(jnp.int32, (lim, N), 0).astype(F32)
    iota_cent = lax.broadcasted_iota(jnp.int32, (lim, L), 1)
    if w % 128 == 0:
        columns = cent[:, pl.ds(pl.multiple_of(r * w, 128), w)]
    else:
        per = 128 // w
        columns = cent[:, pl.ds(pl.multiple_of((r // per) * 128, 128), 128)]

    def fetch(p):
        for j in range(R):
            key = keys[c, pl.ds(j * Cp + p, 1), :]
            idrow = ids_all[j, pl.ds(p, 1), :].astype(F32)
            local = jnp.sum(jnp.where(key == iota_slot, idrow - (c * L).astype(F32), 0.0), axis=1, keepdims=True)
            hot[j * lim:(j + 1) * lim, :] = jnp.where(local.astype(jnp.int32) == iota_cent, 1.0, 0.0).astype(BF16)
        got = dot(hot[...], columns, 1, 0)
        if w % 128:
            own = got[:, 0:w]
            for i in range(1, 128 // w):
                own = jnp.where(lax.rem(r, 128 // w) == i, got[:, i * w:(i + 1) * w], own)
            got = own
        return got.astype(BF16).reshape(R, lim, w)

    order = [d for d in range(2, C - 1)] + ([C - 1] if C > 2 else []) + [1]
    for d in order:
        p = lax.rem(c + d, C)
        comp_send[d] = fetch(p)
        go(remote(comp_send.at[d], comp_recv.at[c], comp_s.at[d], comp_r.at[d], at_cent(p)))
    comp_recv[c] = fetch(c)

    chunk = min(256, L)

    def nearest(j, first):
        rows = qg[pl.ds(2 * j, 2)].reshape(2 * N, D)

        def step(i, best):
            at = pl.ds(pl.multiple_of(i * chunk, chunk), chunk)
            block = cent[at, :]
            if first:
                total = jnp.zeros((chunk, 128), F32)
                for e in range(D // 128):
                    total = total + jnp.square(block[:, e * 128:(e + 1) * 128].astype(F32))
                csq[at, :] = jnp.broadcast_to(jnp.sum(total, axis=1, keepdims=True), (chunk, 128))
            cs = csq[at, :]
            far = jnp.concatenate([cs] * (2 * N // 128), axis=1) - 2.0 * dot(block, rows, 1, 1)
            return jnp.minimum(best, jnp.min(far.reshape(chunk // 8, 8, 2 * N), axis=0))

        best = lax.fori_loop(0, L // chunk, step, jnp.full((8, 2 * N), jnp.inf, F32))
        best = jnp.broadcast_to(jnp.min(best, axis=0, keepdims=True), (8, 2 * N))
        minbuf[2 * j] = best[:, 0:N]
        minbuf[2 * j + 1] = best[:, N:2 * N]

    for e in range(1, half):
        p = lax.rem(c + C - 2 * e, C)
        remote(qg.at[p], qg.at[p], row_s.at[e], row_r.at[e], at_cent(p)).wait_recv()
        go(remote(qg.at[p], qg.at[p], pair_s.at[e], pair_r.at[e], at_cent(partner)))
    remote(qg.at[partner], qg.at[partner], pair_s.at[0], pair_r.at[0], at_cent(partner)).wait_recv()
    nearest(chip, True)

    eye = jnp.where(
        lax.broadcasted_iota(jnp.int32, (N, N), 0) == lax.broadcasted_iota(jnp.int32, (N, N), 1), 1.0, 0.0
    ).astype(BF16)
    for d in range(1, R):
        p = lax.rem(r + R - d, R)
        remote(stage.at[p], deqc.at[p], col_s.at[d], col_r.at[d], at_rows(p)).wait_recv()
    for d in range(1, C):
        p = lax.rem(c + C - d, C)
        remote(comp_send.at[d], comp_recv.at[p], comp_s.at[d], comp_r.at[d], at_cent(p)).wait_recv()
    for j in range(R):
        sel = [
            jnp.where(keys[p, pl.ds(j * Cp + c, 1), :] == iota_slot, 1.0, 0.0).astype(BF16) for p in range(C)
        ]
        got = comp_recv[:, j].reshape(C * lim, w)
        fetched = dot(got, jnp.concatenate(sel, axis=0), 0, 0)
        xt[:, j * N:(j + 1) * N] = dot(deqc[j], eye, 0, 0) - fetched

    wide_rows = xt.shape[1]
    ones = jnp.ones((16, wide_rows), BF16)
    for m in range(msub):
        hi, lo = split(xt[m * sub:(m + 1) * sub, :])
        left = jnp.concatenate([hi, lo, ones], axis=0)
        for t in range(2):
            got = dot(left, oh[t, m], 1, 1)
            total = got[0:sub] + got[sub:2 * sub]
            count = got[2 * sub:2 * sub + 8]
            for h in range(2):
                at = slice(h * (K // 2), (h + 1) * (K // 2))
                st[h, t, m * sub:(m + 1) * sub, :] = total[:, at]
                st[h, t, w + 8 * m:w + 8 * m + 8, :] = count[:, at]

    first = remote(st.at[1 - core], st_in, s1_s, s1_r, at_cent(partner))
    first.start()
    first.wait_recv()
    st_half[chip] = st[core] + st_in[...]
    for e in range(1, half):
        p = lax.rem(c + 2 * e, C)
        go(remote(st_half.at[chip], st_half.at[chip], s2_s.at[e], s2_r.at[e], at_cent(p)))
    for e in range(1, half):
        p = lax.rem(partner + C - 2 * e, C)
        remote(qg.at[p], qg.at[p], pair_s.at[e], pair_r.at[e], at_cent(partner)).wait_recv()
        nearest(lax.rem(chip + half - e, half), False)
    for d in range(1, C):
        p = lax.rem(c + d, C)
        go(remote(minbuf.at[p], minrecv.at[c], min_s.at[d], min_r.at[d], at_cent(p)))
    minrecv[c] = minbuf[c]
    for e in range(1, half):
        p = lax.rem(chip + half - e, half)
        remote(st_half.at[p], st_half.at[p], s2_s.at[e], s2_r.at[e], at_cent(partner)).wait_recv()
    total = st_half[0]
    for e in range(1, half):
        total = total + st_half[e]
    st_out[core] = total
    last = remote(st_out.at[core], st_out.at[core], s3_s, s3_r, at_cent(partner))
    last.start()
    last.wait_send()
    remote(st_out.at[1 - core], st_out.at[1 - core], s3_s, s3_r, at_cent(partner)).wait_recv()

    for m in range(msub):
        at = slice(m * sub, (m + 1) * sub)
        row = slice(w + 8 * m, w + 8 * m + 1)

        def stat(t, rows):
            return jnp.concatenate([st_out[0, t, rows, :], st_out[1, t, rows, :]], axis=1)

        book = init_ref[m].T
        for t, ref in enumerate((book1_ref, book2_ref)):
            book = (stat(t, at) + prior_weight * book) / (stat(t, row) + prior_weight)
            ref[m] = book.T
        hi, lo = split(book)
        made = dot(jnp.concatenate([hi, lo], axis=0), oh[1, m], 1, 0)
        off = xt[at, :] - (made[0:sub] + made[sub:2 * sub])
        dist_ref[m:m + 1, :] = jnp.sum(off * off, axis=0, keepdims=True) * (1.0 / sub)

    for d in range(1, C):
        p = lax.rem(c + C - d, C)
        remote(minbuf.at[p], minrecv.at[p], min_s.at[d], min_r.at[d], at_cent(p)).wait_recv()
    best = minrecv[0]
    for p in range(1, C):
        best = jnp.minimum(best, minrecv[p])
    norm = jnp.broadcast_to(jnp.sum(squares, axis=1, keepdims=True), (N, 128)).T
    gap_ref[...] = (best[0:1] + norm[0:1]) * (1.0 / D)

    first.wait_send()
    for copy in sends:
        copy.wait_send()


def on_device(C, R, emb_values, emb_scales, coarse_ids, centroids, codes_one, codes_two, codebook_init):
    N, D = emb_values.shape
    L = centroids.shape[0]
    msub, K, sub = codebook_init.shape
    w = msub * sub
    lim = 2 * N // C
    Cp = max(8, C)
    rows = codes_one.shape[1]
    tall = w + 8 * msub
    vmem = pl.BlockSpec(memory_space=pltpu.VMEM)
    dma = pltpu.SemaphoreType.DMA
    gap, book_one, book_two, distortion = pl.pallas_call(
        functools.partial(kernel, C, R),
        out_shape=(
            jax.ShapeDtypeStruct((1, N), F32),
            jax.ShapeDtypeStruct((msub, K, sub), F32),
            jax.ShapeDtypeStruct((msub, K, sub), F32),
            jax.ShapeDtypeStruct((msub, rows), F32),
        ),
        in_specs=[vmem, vmem, vmem, pl.BlockSpec(memory_space=pl.ANY), vmem, vmem, vmem],
        out_specs=(vmem,) * 4,
        scratch_shapes=[
            pltpu.VMEM((L, D), BF16),
            pltpu.VMEM((C, N, D), BF16),
            pltpu.VMEM((R, N, w), BF16),
            pltpu.VMEM((R, N, w), BF16),
            pltpu.VMEM((Cp, N), jnp.int32),
            pltpu.VMEM((R, Cp, N), jnp.int32),
            pltpu.VMEM((C, R * Cp, N), F32),
            pltpu.VMEM((R * lim, L), BF16),
            pltpu.VMEM((C, R, lim, w), BF16),
            pltpu.VMEM((C, R, lim, w), BF16),
            pltpu.VMEM((L, 128), F32),
            pltpu.VMEM((C, 8, N), F32),
            pltpu.VMEM((C, 8, N), F32),
            pltpu.VMEM((w, rows), F32),
            pltpu.VMEM((2, msub, K, rows), BF16),
            pltpu.VMEM((2, 2, tall, K // 2), F32),
            pltpu.VMEM((2, tall, K // 2), F32),
            pltpu.VMEM((C // 2, 2, tall, K // 2), F32),
            pltpu.VMEM((2, 2, tall, K // 2), F32),
            dma,
            dma((R,)), dma((R,)), dma((R,)), dma((R,)),
            dma((C // 2,)), dma((C // 2,)), dma((C // 2,)), dma((C // 2,)),
            dma((C,)), dma((C,)), dma((C,)), dma((C,)),
            dma, dma,
            dma((C // 2,)), dma((C // 2,)),
            dma, dma,
        ],
        compiler_params=pltpu.CompilerParams(
            collective_id=0, has_side_effects=True, vmem_limit_bytes=48 * 1024 * 1024
        ),
    )(emb_values, emb_scales, coarse_ids, centroids, codes_one, codes_two, codebook_init)
    return gap.reshape(N), book_one, book_two, distortion


def solution(mesh):
    placed = (
        P(("cent", "rows"), None),
        P(("cent", "rows"), None),
        P(None, "rows"),
        P("cent", None),
        P("rows", "cent"),
        P("rows", "cent"),
        P("rows", None, None),
    )
    return jax.shard_map(
        functools.partial(on_device, mesh.shape["cent"], mesh.shape["rows"]),
        mesh=mesh,
        in_specs=placed,
        out_specs=(
            P(("cent", "rows")),
            P("rows", None, None),
            P("rows", None, None),
            P("rows", "cent"),
        ),
        check_vma=False,
    )
```

```python
import functools

import jax
import jax.numpy as jnp
from jax import lax
from jax.experimental import pallas as pl
from jax.experimental.pallas import tpu as pltpu
from jax.sharding import PartitionSpec as P

prior_weight = 8.0
MESH = pl.DeviceIdType.MESH
F32, BF16 = jnp.float32, jnp.bfloat16


def dot(a, b, ca, cb):
    return lax.dot_general(a, b, (((ca,), (cb,)), ((), ())), preferred_element_type=F32)


def split(x):
    hi = x.astype(BF16)
    return hi, (x - hi.astype(F32)).astype(BF16)


def kernel(
    C, R,
    val_hbm, scale_hbm, ids_hbm, cent_hbm, one_hbm, two_hbm, init_hbm,
    gap_ref, book1_ref, book2_ref, dist_ref,
    val_ref, scale_ref, ids_ref, one_ref, two_ref, init_ref,
    cent, qg, stage, deqc, ids_pad, ids_all, keys, hot, comp_send, comp_recv,
    csq, minbuf, minrecv, xt, oh, st, st_in, st_half, st_out,
    in_sem, cent_sem, ids_s, ids_r, col_s, col_r, row_s, row_r, pair_s, pair_r,
    comp_s, comp_r, min_s, min_r, s1_s, s1_r, s2_s, s2_r, s3_s, s3_r,
):
    r, c = lax.axis_index("rows"), lax.axis_index("cent")
    N, D = val_ref.shape
    L = cent.shape[0]
    w = stage.shape[2]
    msub = one_ref.shape[0]
    sub = w // msub
    K = init_ref.shape[2]
    lim = comp_send.shape[2]
    Cp = ids_pad.shape[0]
    half = C // 2
    core = lax.rem(c, 2)
    partner = c + 1 - 2 * core
    chip = c // 2

    def at_cent(p):
        return (r, p)

    def at_rows(p):
        return (p, c)

    def remote(src, dst, s, rr, dev):
        return pltpu.make_async_remote_copy(
            src_ref=src, dst_ref=dst, send_sem=s, recv_sem=rr, device_id=dev, device_id_type=MESH
        )

    loads = [
        pltpu.make_async_copy(src, dst, in_sem.at[i])
        for i, (src, dst) in enumerate((
            (val_hbm, val_ref), (scale_hbm, scale_ref), (ids_hbm, ids_ref),
            (one_hbm, one_ref), (two_hbm, two_ref), (init_hbm, init_ref),
        ))
    ]
    for copy in loads:
        copy.start()
    load = pltpu.make_async_copy(cent_hbm, cent, cent_sem)
    load.start()
    barrier = pltpu.get_barrier_semaphore()
    for d in range(1, C):
        pl.semaphore_signal(barrier, inc=1, device_id=at_cent(lax.rem(c + d, C)), device_id_type=MESH)
    for d in range(1, R):
        pl.semaphore_signal(barrier, inc=1, device_id=at_rows(lax.rem(r + d, R)), device_id_type=MESH)

    blocks = scale_ref.shape[0]
    width = D // blocks
    spread = jnp.where(
        lax.broadcasted_iota(jnp.int32, (blocks, D), 1) // width
        == lax.broadcasted_iota(jnp.int32, (blocks, D), 0), 1.0, 0.0
    ).astype(BF16)
    for copy in loads[:3]:
        copy.wait()
    scales = dot(scale_ref[...], spread, 0, 0)
    squares = jnp.zeros((N, 128), F32)
    for b in range(D // width):
        part = val_ref[:, b * width:(b + 1) * width].astype(F32) * scales[:, b * width:(b + 1) * width]
        part = part.astype(BF16)
        qg[c, :, b * width:(b + 1) * width] = part
        wide = part.astype(F32)
        for e in range(width // 128):
            squares = squares + jnp.square(wide[:, e * 128:(e + 1) * 128])
    for j in range(R):
        stage[j] = qg[c, :, j * w:(j + 1) * w]
    ids_pad[...] = jnp.full(ids_pad.shape, -1, jnp.int32)
    ids_pad[0:C] = ids_ref[...]
    ids_all[r] = ids_pad[...]
    deqc[r] = stage[r]

    pl.semaphore_wait(barrier, C - 1 + R - 1)

    sends = []

    def go(copy):
        copy.start()
        sends.append(copy)

    for d in range(1, R):
        p = lax.rem(r + d, R)
        go(remote(ids_pad, ids_all.at[r], ids_s.at[d], ids_r.at[d], at_rows(p)))
    for e in range(1, half):
        p = lax.rem(c + 2 * e, C)
        go(remote(qg.at[c], qg.at[c], row_s.at[e], row_r.at[e], at_cent(p)))
    go(remote(qg.at[c], qg.at[c], pair_s.at[0], pair_r.at[0], at_cent(partner)))
    for d in range(1, R):
        p = lax.rem(r + d, R)
        go(remote(stage.at[p], deqc.at[r], col_s.at[d], col_r.at[d], at_rows(p)))

    for d in range(1, R):
        p = lax.rem(r + R - d, R)
        remote(ids_pad, ids_all.at[p], ids_s.at[d], ids_r.at[d], at_rows(p)).wait_recv()
    ids = ids_all[...].reshape(R * Cp, N)
    before = jnp.where(
        lax.broadcasted_iota(jnp.int32, (N, N), 0) < lax.broadcasted_iota(jnp.int32, (N, N), 1), 1.0, 0.0
    ).astype(BF16)
    for p in range(C):
        mask = (ids >= p * L) & (ids < (p + 1) * L)
        rank = dot(jnp.where(mask, 1.0, 0.0).astype(BF16), before, 1, 0)
        keys[p] = jnp.where(mask, rank, -1.0)

    load.wait()
    iota_slot = lax.broadcasted_iota(jnp.int32, (lim, N), 0).astype(F32)
    iota_cent = lax.broadcasted_iota(jnp.int32, (lim, L), 1)
    if w % 128 == 0:
        columns = cent[:, pl.ds(pl.multiple_of(r * w, 128), w)]
    else:
        per = 128 // w
        columns = cent[:, pl.ds(pl.multiple_of((r // per) * 128, 128), 128)]

    def fetch(p):
        for j in range(R):
            key = keys[c, pl.ds(j * Cp + p, 1), :]
            idrow = ids_all[j, pl.ds(p, 1), :].astype(F32)
            local = jnp.sum(jnp.where(key == iota_slot, idrow - (c * L).astype(F32), 0.0), axis=1, keepdims=True)
            hot[j * lim:(j + 1) * lim, :] = jnp.where(local.astype(jnp.int32) == iota_cent, 1.0, 0.0).astype(BF16)
        got = dot(hot[...], columns, 1, 0)
        if w % 128:
            own = got[:, 0:w]
            for i in range(1, 128 // w):
                own = jnp.where(lax.rem(r, 128 // w) == i, got[:, i * w:(i + 1) * w], own)
            got = own
        return got.astype(BF16).reshape(R, lim, w)

    order = [d for d in range(2, C - 1)] + ([C - 1] if C > 2 else []) + [1]
    for d in order:
        p = lax.rem(c + d, C)
        comp_send[d] = fetch(p)
        go(remote(comp_send.at[d], comp_recv.at[c], comp_s.at[d], comp_r.at[d], at_cent(p)))
    comp_recv[c] = fetch(c)

    for copy in loads[3:]:
        copy.wait()
    iota_k = lax.broadcasted_iota(jnp.int32, (K, one_ref.shape[1]), 0)
    for t, ref in enumerate((one_ref, two_ref)):
        for m in range(msub):
            oh[t, m] = jnp.where(ref[m:m + 1, :] == iota_k, 1.0, 0.0).astype(BF16)

    chunk = min(256, L)

    def nearest(j, first):
        rows = qg[pl.ds(2 * j, 2)].reshape(2 * N, D)

        def step(i, best):
            at = pl.ds(pl.multiple_of(i * chunk, chunk), chunk)
            block = cent[at, :]
            if first:
                total = jnp.zeros((chunk, 128), F32)
                for e in range(D // 128):
                    total = total + jnp.square(block[:, e * 128:(e + 1) * 128].astype(F32))
                csq[at, :] = jnp.broadcast_to(jnp.sum(total, axis=1, keepdims=True), (chunk, 128))
            cs = csq[at, :]
            far = jnp.concatenate([cs] * (2 * N // 128), axis=1) - 2.0 * dot(block, rows, 1, 1)
            return jnp.minimum(best, jnp.min(far.reshape(chunk // 8, 8, 2 * N), axis=0))

        best = lax.fori_loop(0, L // chunk, step, jnp.full((8, 2 * N), jnp.inf, F32))
        best = jnp.broadcast_to(jnp.min(best, axis=0, keepdims=True), (8, 2 * N))
        minbuf[2 * j] = best[:, 0:N]
        minbuf[2 * j + 1] = best[:, N:2 * N]

    for e in range(1, half):
        p = lax.rem(c + C - 2 * e, C)
        remote(qg.at[p], qg.at[p], row_s.at[e], row_r.at[e], at_cent(p)).wait_recv()
        go(remote(qg.at[p], qg.at[p], pair_s.at[e], pair_r.at[e], at_cent(partner)))
    remote(qg.at[partner], qg.at[partner], pair_s.at[0], pair_r.at[0], at_cent(partner)).wait_recv()
    nearest(chip, True)

    eye = jnp.where(
        lax.broadcasted_iota(jnp.int32, (N, N), 0) == lax.broadcasted_iota(jnp.int32, (N, N), 1), 1.0, 0.0
    ).astype(BF16)
    for d in range(1, R):
        p = lax.rem(r + R - d, R)
        remote(stage.at[p], deqc.at[p], col_s.at[d], col_r.at[d], at_rows(p)).wait_recv()
    for d in range(1, C):
        p = lax.rem(c + C - d, C)
        remote(comp_send.at[d], comp_recv.at[p], comp_s.at[d], comp_r.at[d], at_cent(p)).wait_recv()
    for j in range(R):
        sel = [
            jnp.where(keys[p, pl.ds(j * Cp + c, 1), :] == iota_slot, 1.0, 0.0).astype(BF16) for p in range(C)
        ]
        got = comp_recv[:, j].reshape(C * lim, w)
        fetched = dot(got, jnp.concatenate(sel, axis=0), 0, 0)
        xt[:, j * N:(j + 1) * N] = dot(deqc[j], eye, 0, 0) - fetched

    wide_rows = xt.shape[1]
    ones = jnp.ones((16, wide_rows), BF16)
    for m in range(msub):
        hi, lo = split(xt[m * sub:(m + 1) * sub, :])
        left = jnp.concatenate([hi, lo, ones], axis=0)
        for t in range(2):
            got = dot(left, oh[t, m], 1, 1)
            total = got[0:sub] + got[sub:2 * sub]
            count = got[2 * sub:2 * sub + 8]
            for h in range(2):
                at = slice(h * (K // 2), (h + 1) * (K // 2))
                st[h, t, m * sub:(m + 1) * sub, :] = total[:, at]
                st[h, t, w + 8 * m:w + 8 * m + 8, :] = count[:, at]

    first = remote(st.at[1 - core], st_in, s1_s, s1_r, at_cent(partner))
    first.start()
    first.wait_recv()
    st_half[chip] = st[core] + st_in[...]
    for e in range(1, half):
        p = lax.rem(c + 2 * e, C)
        go(remote(st_half.at[chip], st_half.at[chip], s2_s.at[e], s2_r.at[e], at_cent(p)))
    for e in range(1, half):
        p = lax.rem(partner + C - 2 * e, C)
        remote(qg.at[p], qg.at[p], pair_s.at[e], pair_r.at[e], at_cent(partner)).wait_recv()
        nearest(lax.rem(chip + half - e, half), False)
    for d in range(1, C):
        p = lax.rem(c + d, C)
        go(remote(minbuf.at[p], minrecv.at[c], min_s.at[d], min_r.at[d], at_cent(p)))
    minrecv[c] = minbuf[c]
    for e in range(1, half):
        p = lax.rem(chip + half - e, half)
        remote(st_half.at[p], st_half.at[p], s2_s.at[e], s2_r.at[e], at_cent(partner)).wait_recv()
    total = st_half[0]
    for e in range(1, half):
        total = total + st_half[e]
    st_out[core] = total
    last = remote(st_out.at[core], st_out.at[core], s3_s, s3_r, at_cent(partner))
    last.start()
    last.wait_send()
    remote(st_out.at[1 - core], st_out.at[1 - core], s3_s, s3_r, at_cent(partner)).wait_recv()

    for m in range(msub):
        at = slice(m * sub, (m + 1) * sub)
        row = slice(w + 8 * m, w + 8 * m + 1)

        def stat(t, rows):
            return jnp.concatenate([st_out[0, t, rows, :], st_out[1, t, rows, :]], axis=1)

        book = init_ref[m]
        for t, ref in enumerate((book1_ref, book2_ref)):
            book = (stat(t, at) + prior_weight * book) / (stat(t, row) + prior_weight)
            ref[m] = book
        hi, lo = split(book)
        made = dot(jnp.concatenate([hi, lo], axis=0), oh[1, m], 1, 0)
        off = xt[at, :] - (made[0:sub] + made[sub:2 * sub])
        dist_ref[m:m + 1, :] = jnp.sum(off * off, axis=0, keepdims=True) * (1.0 / sub)

    for d in range(1, C):
        p = lax.rem(c + C - d, C)
        remote(minbuf.at[p], minrecv.at[p], min_s.at[d], min_r.at[d], at_cent(p)).wait_recv()
    best = minrecv[0]
    for p in range(1, C):
        best = jnp.minimum(best, minrecv[p])
    norm = jnp.broadcast_to(jnp.sum(squares, axis=1, keepdims=True), (N, 128)).T
    gap_ref[...] = (best[0:1] + norm[0:1]) * (1.0 / D)

    first.wait_send()
    for copy in sends:
        copy.wait_send()


def write_out(a0, a1, a2, a3, b0, b1, b2, b3, sems):
    copies = [
        pltpu.make_async_copy(a, b, sems.at[i]) for i, (a, b) in enumerate(((a0, b0), (a1, b1), (a2, b2), (a3, b3)))
    ]
    for copy in copies:
        copy.start()
    for copy in copies:
        copy.wait()


def on_device(C, R, emb_values, emb_scales, coarse_ids, centroids, codes_one, codes_two, codebook_init):
    N, D = emb_values.shape
    L = centroids.shape[0]
    msub, K, sub = codebook_init.shape
    blocks = emb_scales.shape[1]
    w = msub * sub
    lim = 2 * N // C
    Cp = max(8, C)
    rows = codes_one.shape[1]
    tall = w + 8 * msub
    vmem = pl.BlockSpec(memory_space=pltpu.VMEM)
    hbm = pl.BlockSpec(memory_space=pltpu.HBM)
    dma = pltpu.SemaphoreType.DMA
    results = pl.pallas_call(
        functools.partial(kernel, C, R),
        out_shape=(
            jax.ShapeDtypeStruct((1, N), F32),
            jax.ShapeDtypeStruct((msub, sub, K), F32),
            jax.ShapeDtypeStruct((msub, sub, K), F32),
            jax.ShapeDtypeStruct((msub, rows), F32),
        ),
        in_specs=[hbm] * 7,
        out_specs=(vmem,) * 4,
        scratch_shapes=[
            pltpu.VMEM((N, D), BF16),
            pltpu.VMEM((blocks, N), BF16),
            pltpu.VMEM((C, N), jnp.int32),
            pltpu.VMEM((msub, rows), jnp.int32),
            pltpu.VMEM((msub, rows), jnp.int32),
            pltpu.VMEM((msub, sub, K), F32),
            pltpu.VMEM((L, D), BF16),
            pltpu.VMEM((C, N, D), BF16),
            pltpu.VMEM((R, N, w), BF16),
            pltpu.VMEM((R, N, w), BF16),
            pltpu.VMEM((Cp, N), jnp.int32),
            pltpu.VMEM((R, Cp, N), jnp.int32),
            pltpu.VMEM((C, R * Cp, N), F32),
            pltpu.VMEM((R * lim, L), BF16),
            pltpu.VMEM((C, R, lim, w), BF16),
            pltpu.VMEM((C, R, lim, w), BF16),
            pltpu.VMEM((L, 128), F32),
            pltpu.VMEM((C, 8, N), F32),
            pltpu.VMEM((C, 8, N), F32),
            pltpu.VMEM((w, rows), F32),
            pltpu.VMEM((2, msub, K, rows), BF16),
            pltpu.VMEM((2, 2, tall, K // 2), F32),
            pltpu.VMEM((2, tall, K // 2), F32),
            pltpu.VMEM((C // 2, 2, tall, K // 2), F32),
            pltpu.VMEM((2, 2, tall, K // 2), F32),
            dma((6,)), dma,
            dma((R,)), dma((R,)), dma((R,)), dma((R,)),
            dma((C // 2,)), dma((C // 2,)), dma((C // 2,)), dma((C // 2,)),
            dma((C,)), dma((C,)), dma((C,)), dma((C,)),
            dma, dma,
            dma((C // 2,)), dma((C // 2,)),
            dma, dma,
        ],
        compiler_params=pltpu.CompilerParams(
            collective_id=0, has_side_effects=True, vmem_limit_bytes=60 * 1024 * 1024
        ),
    )(
        emb_values, emb_scales.T, coarse_ids, centroids, codes_one, codes_two,
        jnp.swapaxes(codebook_init, 1, 2),
    )
    gap, book_one, book_two, distortion = pl.pallas_call(
        write_out,
        out_shape=tuple(jax.ShapeDtypeStruct(a.shape, a.dtype) for a in results),
        in_specs=[pl.BlockSpec(memory_space=pl.ANY)] * 4,
        out_specs=(hbm,) * 4,
        scratch_shapes=[dma((4,))],
    )(*results)
    return gap.reshape(N), jnp.swapaxes(book_one, 1, 2), jnp.swapaxes(book_two, 1, 2), distortion


def solution(mesh):
    placed = (
        P(("cent", "rows"), None),
        P(("cent", "rows"), None),
        P(None, "rows"),
        P("cent", None),
        P("rows", "cent"),
        P("rows", "cent"),
        P("rows", None, None),
    )
    return jax.shard_map(
        functools.partial(on_device, mesh.shape["cent"], mesh.shape["rows"]),
        mesh=mesh,
        in_specs=placed,
        out_specs=(
            P(("cent", "rows")),
            P("rows", None, None),
            P("rows", None, None),
            P("rows", "cent"),
        ),
        check_vma=False,
    )
```

```python
import functools

import jax
import jax.numpy as jnp
from jax import lax
from jax.experimental import pallas as pl
from jax.experimental.pallas import tpu as pltpu
from jax.sharding import PartitionSpec as P

prior_weight = 8.0
MESH = pl.DeviceIdType.MESH
F32, BF16 = jnp.float32, jnp.bfloat16


def dot(a, b, ca, cb):
    return lax.dot_general(a, b, (((ca,), (cb,)), ((), ())), preferred_element_type=F32)


def split(x):
    hi = x.astype(BF16)
    return hi, (x - hi.astype(F32)).astype(BF16)


def kernel(
    C, R,
    val_hbm, scale_hbm, ids_hbm, cent_hbm, one_hbm, two_hbm, init_hbm,
    gap_ref, book1_ref, book2_ref, dist_ref,
    val_ref, scale_ref, ids_ref, one_ref, two_ref, init_ref,
    cent, qg, stage, deqc, ids_pad, ids_all, keys, hot, comp_send, comp_recv,
    csq, minbuf, minrecv, xt, oh, st, st_in, st_half, st_out,
    in_sem, cent_sem, ids_s, ids_r, col_s, col_r, row_s, row_r, pair_s, pair_r,
    comp_s, comp_r, min_s, min_r, s1_s, s1_r, s2_s, s2_r, s3_s, s3_r,
):
    r, c = lax.axis_index("rows"), lax.axis_index("cent")
    N, D = val_ref.shape
    L = cent.shape[0]
    w = stage.shape[2]
    msub = one_ref.shape[0]
    sub = w // msub
    K = init_ref.shape[2]
    lim = comp_send.shape[2]
    Cp = ids_pad.shape[0]
    half = C // 2
    core = lax.rem(c, 2)
    partner = c + 1 - 2 * core
    chip = c // 2

    def at_cent(p):
        return (r, p)

    def at_rows(p):
        return (p, c)

    def remote(src, dst, s, rr, dev):
        return pltpu.make_async_remote_copy(
            src_ref=src, dst_ref=dst, send_sem=s, recv_sem=rr, device_id=dev, device_id_type=MESH
        )

    loads = [
        pltpu.make_async_copy(src, dst, in_sem.at[i])
        for i, (src, dst) in enumerate((
            (val_hbm, val_ref), (scale_hbm, scale_ref), (ids_hbm, ids_ref),
            (one_hbm, one_ref), (two_hbm, two_ref), (init_hbm, init_ref),
        ))
    ]
    for copy in loads:
        copy.start()
    load = pltpu.make_async_copy(cent_hbm, cent, cent_sem)
    load.start()
    barrier = pltpu.get_barrier_semaphore()
    for d in range(1, C):
        pl.semaphore_signal(barrier, inc=1, device_id=at_cent(lax.rem(c + d, C)), device_id_type=MESH)
    for d in range(1, R):
        pl.semaphore_signal(barrier, inc=1, device_id=at_rows(lax.rem(r + d, R)), device_id_type=MESH)

    blocks = scale_ref.shape[0]
    width = D // blocks
    spread = jnp.where(
        lax.broadcasted_iota(jnp.int32, (blocks, D), 1) // width
        == lax.broadcasted_iota(jnp.int32, (blocks, D), 0), 1.0, 0.0
    ).astype(BF16)
    for copy in loads[:3]:
        copy.wait()
    scales = dot(scale_ref[...], spread, 0, 0)
    squares = jnp.zeros((N, 128), F32)
    for b in range(D // width):
        part = val_ref[:, b * width:(b + 1) * width].astype(F32) * scales[:, b * width:(b + 1) * width]
        part = part.astype(BF16)
        qg[c, :, b * width:(b + 1) * width] = part
        wide = part.astype(F32)
        for e in range(width // 128):
            squares = squares + jnp.square(wide[:, e * 128:(e + 1) * 128])
    for j in range(R):
        stage[j] = qg[c, :, j * w:(j + 1) * w]
    ids_pad[...] = jnp.full(ids_pad.shape, -1, jnp.int32)
    ids_pad[0:C] = ids_ref[...]
    ids_all[r] = ids_pad[...]
    deqc[r] = stage[r]

    pl.semaphore_wait(barrier, C - 1 + R - 1)

    sends = []

    def go(copy):
        copy.start()
        sends.append(copy)

    for d in range(1, R):
        p = lax.rem(r + d, R)
        go(remote(ids_pad, ids_all.at[r], ids_s.at[d], ids_r.at[d], at_rows(p)))
    for e in range(1, half):
        p = lax.rem(c + 2 * e, C)
        go(remote(qg.at[c], qg.at[c], row_s.at[e], row_r.at[e], at_cent(p)))
    go(remote(qg.at[c], qg.at[c], pair_s.at[0], pair_r.at[0], at_cent(partner)))
    for d in range(1, R):
        p = lax.rem(r + d, R)
        go(remote(stage.at[p], deqc.at[r], col_s.at[d], col_r.at[d], at_rows(p)))

    for d in range(1, R):
        p = lax.rem(r + R - d, R)
        remote(ids_pad, ids_all.at[p], ids_s.at[d], ids_r.at[d], at_rows(p)).wait_recv()
    ids = ids_all[...].reshape(R * Cp, N)
    before = jnp.where(
        lax.broadcasted_iota(jnp.int32, (N, N), 0) < lax.broadcasted_iota(jnp.int32, (N, N), 1), 1.0, 0.0
    ).astype(BF16)
    for p in range(C):
        mask = (ids >= p * L) & (ids < (p + 1) * L)
        rank = dot(jnp.where(mask, 1.0, 0.0).astype(BF16), before, 1, 0)
        keys[p] = jnp.where(mask, rank, -1.0)

    load.wait()
    iota_slot = lax.broadcasted_iota(jnp.int32, (lim, N), 0).astype(F32)
    iota_cent = lax.broadcasted_iota(jnp.int32, (lim, L), 1)
    if w % 128 == 0:
        columns = cent[:, pl.ds(pl.multiple_of(r * w, 128), w)]
    else:
        per = 128 // w
        columns = cent[:, pl.ds(pl.multiple_of((r // per) * 128, 128), 128)]

    def fetch(p):
        for j in range(R):
            key = keys[c, pl.ds(j * Cp + p, 1), :]
            idrow = ids_all[j, pl.ds(p, 1), :].astype(F32)
            local = jnp.sum(jnp.where(key == iota_slot, idrow - (c * L).astype(F32), 0.0), axis=1, keepdims=True)
            hot[j * lim:(j + 1) * lim, :] = jnp.where(local.astype(jnp.int32) == iota_cent, 1.0, 0.0).astype(BF16)
        got = dot(hot[...], columns, 1, 0)
        if w % 128:
            own = got[:, 0:w]
            for i in range(1, 128 // w):
                own = jnp.where(lax.rem(r, 128 // w) == i, got[:, i * w:(i + 1) * w], own)
            got = own
        return got.astype(BF16).reshape(R, lim, w)

    order = [d for d in range(2, C - 1)] + ([C - 1] if C > 2 else []) + [1]
    for d in order:
        p = lax.rem(c + d, C)
        comp_send[d] = fetch(p)
        go(remote(comp_send.at[d], comp_recv.at[c], comp_s.at[d], comp_r.at[d], at_cent(p)))
    comp_recv[c] = fetch(c)

    for copy in loads[3:]:
        copy.wait()
    iota_k = lax.broadcasted_iota(jnp.int32, (K, one_ref.shape[1]), 0)
    for t, ref in enumerate((one_ref, two_ref)):
        for m in range(msub):
            oh[t, m] = jnp.where(ref[m:m + 1, :] == iota_k, 1.0, 0.0).astype(BF16)

    chunk = min(256, L)

    def nearest(j, first):
        rows = qg[pl.ds(2 * j, 2)].reshape(2 * N, D)

        def step(i, best):
            at = pl.ds(pl.multiple_of(i * chunk, chunk), chunk)
            block = cent[at, :]
            if first:
                total = jnp.zeros((chunk, 128), F32)
                for e in range(D // 128):
                    total = total + jnp.square(block[:, e * 128:(e + 1) * 128].astype(F32))
                csq[at, :] = jnp.broadcast_to(jnp.sum(total, axis=1, keepdims=True), (chunk, 128))
            cs = csq[at, :]
            far = jnp.concatenate([cs] * (2 * N // 128), axis=1) - 2.0 * dot(block, rows, 1, 1)
            return jnp.minimum(best, jnp.min(far.reshape(chunk // 8, 8, 2 * N), axis=0))

        best = lax.fori_loop(0, L // chunk, step, jnp.full((8, 2 * N), jnp.inf, F32))
        best = jnp.broadcast_to(jnp.min(best, axis=0, keepdims=True), (8, 2 * N))
        minbuf[2 * j] = best[:, 0:N]
        minbuf[2 * j + 1] = best[:, N:2 * N]

    for e in range(1, half):
        p = lax.rem(c + C - 2 * e, C)
        remote(qg.at[p], qg.at[p], row_s.at[e], row_r.at[e], at_cent(p)).wait_recv()
        go(remote(qg.at[p], qg.at[p], pair_s.at[e], pair_r.at[e], at_cent(partner)))
    remote(qg.at[partner], qg.at[partner], pair_s.at[0], pair_r.at[0], at_cent(partner)).wait_recv()
    nearest(chip, True)

    eye = jnp.where(
        lax.broadcasted_iota(jnp.int32, (N, N), 0) == lax.broadcasted_iota(jnp.int32, (N, N), 1), 1.0, 0.0
    ).astype(BF16)
    for d in range(1, R):
        p = lax.rem(r + R - d, R)
        remote(stage.at[p], deqc.at[p], col_s.at[d], col_r.at[d], at_rows(p)).wait_recv()
    for d in range(1, C):
        p = lax.rem(c + C - d, C)
        remote(comp_send.at[d], comp_recv.at[p], comp_s.at[d], comp_r.at[d], at_cent(p)).wait_recv()
    for j in range(R):
        sel = [
            jnp.where(keys[p, pl.ds(j * Cp + c, 1), :] == iota_slot, 1.0, 0.0).astype(BF16) for p in range(C)
        ]
        got = comp_recv[:, j].reshape(C * lim, w)
        fetched = dot(got, jnp.concatenate(sel, axis=0), 0, 0)
        xt[:, j * N:(j + 1) * N] = dot(deqc[j], eye, 0, 0) - fetched

    wide_rows = xt.shape[1]
    ones = jnp.ones((16, wide_rows), BF16)
    for m in range(msub):
        hi, lo = split(xt[m * sub:(m + 1) * sub, :])
        left = jnp.concatenate([hi, lo, ones], axis=0)
        for t in range(2):
            got = dot(left, oh[t, m], 1, 1)
            total = got[0:sub] + got[sub:2 * sub]
            count = got[2 * sub:2 * sub + 8]
            for h in range(2):
                at = slice(h * (K // 2), (h + 1) * (K // 2))
                st[h, t, m * sub:(m + 1) * sub, :] = total[:, at]
                st[h, t, w + 8 * m:w + 8 * m + 8, :] = count[:, at]

    first = remote(st.at[1 - core], st_in, s1_s, s1_r, at_cent(partner))
    first.start()
    first.wait_recv()
    st_half[chip] = st[core] + st_in[...]
    for e in range(1, half):
        p = lax.rem(c + 2 * e, C)
        go(remote(st_half.at[chip], st_half.at[chip], s2_s.at[e], s2_r.at[e], at_cent(p)))
    for e in range(1, half):
        p = lax.rem(partner + C - 2 * e, C)
        remote(qg.at[p], qg.at[p], pair_s.at[e], pair_r.at[e], at_cent(partner)).wait_recv()
        nearest(lax.rem(chip + half - e, half), False)
    for d in range(1, C):
        p = lax.rem(c + d, C)
        go(remote(minbuf.at[p], minrecv.at[c], min_s.at[d], min_r.at[d], at_cent(p)))
    minrecv[c] = minbuf[c]
    for e in range(1, half):
        p = lax.rem(chip + half - e, half)
        remote(st_half.at[p], st_half.at[p], s2_s.at[e], s2_r.at[e], at_cent(partner)).wait_recv()
    total = st_half[0]
    for e in range(1, half):
        total = total + st_half[e]
    st_out[core] = total
    last = remote(st_out.at[core], st_out.at[core], s3_s, s3_r, at_cent(partner))
    last.start()
    last.wait_send()
    remote(st_out.at[1 - core], st_out.at[1 - core], s3_s, s3_r, at_cent(partner)).wait_recv()

    for m in range(msub):
        at = slice(m * sub, (m + 1) * sub)
        row = slice(w + 8 * m, w + 8 * m + 1)

        def stat(t, rows):
            return jnp.concatenate([st_out[0, t, rows, :], st_out[1, t, rows, :]], axis=1)

        book = init_ref[m]
        for t, ref in enumerate((book1_ref, book2_ref)):
            book = (stat(t, at) + prior_weight * book) / (stat(t, row) + prior_weight)
            ref[m] = book
        hi, lo = split(book)
        made = dot(jnp.concatenate([hi, lo], axis=0), oh[1, m], 1, 0)
        off = xt[at, :] - (made[0:sub] + made[sub:2 * sub])
        dist_ref[m:m + 1, :] = jnp.sum(off * off, axis=0, keepdims=True) * (1.0 / sub)

    for d in range(1, C):
        p = lax.rem(c + C - d, C)
        remote(minbuf.at[p], minrecv.at[p], min_s.at[d], min_r.at[d], at_cent(p)).wait_recv()
    best = minrecv[0]
    for p in range(1, C):
        best = jnp.minimum(best, minrecv[p])
    norm = jnp.broadcast_to(jnp.sum(squares, axis=1, keepdims=True), (N, 128)).T
    gap_ref[...] = (best[0:1] + norm[0:1]) * (1.0 / D)

    first.wait_send()
    for copy in sends:
        copy.wait_send()


def write_out(*refs):
    for src, dst in zip(refs[:4], refs[4:]):
        dst[...] = src[...]


def on_device(C, R, emb_values, emb_scales, coarse_ids, centroids, codes_one, codes_two, codebook_init):
    N, D = emb_values.shape
    L = centroids.shape[0]
    msub, K, sub = codebook_init.shape
    blocks = emb_scales.shape[1]
    w = msub * sub
    lim = 2 * N // C
    Cp = max(8, C)
    rows = codes_one.shape[1]
    tall = w + 8 * msub
    vmem = pl.BlockSpec(memory_space=pltpu.VMEM)
    hbm = pl.BlockSpec(memory_space=pltpu.HBM)
    dma = pltpu.SemaphoreType.DMA
    results = pl.pallas_call(
        functools.partial(kernel, C, R),
        out_shape=(
            jax.ShapeDtypeStruct((1, N), F32),
            jax.ShapeDtypeStruct((msub, sub, K), F32),
            jax.ShapeDtypeStruct((msub, sub, K), F32),
            jax.ShapeDtypeStruct((msub, rows), F32),
        ),
        in_specs=[hbm] * 7,
        out_specs=(vmem,) * 4,
        scratch_shapes=[
            pltpu.VMEM((N, D), BF16),
            pltpu.VMEM((blocks, N), BF16),
            pltpu.VMEM((C, N), jnp.int32),
            pltpu.VMEM((msub, rows), jnp.int32),
            pltpu.VMEM((msub, rows), jnp.int32),
            pltpu.VMEM((msub, sub, K), F32),
            pltpu.VMEM((L, D), BF16),
            pltpu.VMEM((C, N, D), BF16),
            pltpu.VMEM((R, N, w), BF16),
            pltpu.VMEM((R, N, w), BF16),
            pltpu.VMEM((Cp, N), jnp.int32),
            pltpu.VMEM((R, Cp, N), jnp.int32),
            pltpu.VMEM((C, R * Cp, N), F32),
            pltpu.VMEM((R * lim, L), BF16),
            pltpu.VMEM((C, R, lim, w), BF16),
            pltpu.VMEM((C, R, lim, w), BF16),
            pltpu.VMEM((L, 128), F32),
            pltpu.VMEM((C, 8, N), F32),
            pltpu.VMEM((C, 8, N), F32),
            pltpu.VMEM((w, rows), F32),
            pltpu.VMEM((2, msub, K, rows), BF16),
            pltpu.VMEM((2, 2, tall, K // 2), F32),
            pltpu.VMEM((2, tall, K // 2), F32),
            pltpu.VMEM((C // 2, 2, tall, K // 2), F32),
            pltpu.VMEM((2, 2, tall, K // 2), F32),
            dma((6,)), dma,
            dma((R,)), dma((R,)), dma((R,)), dma((R,)),
            dma((C // 2,)), dma((C // 2,)), dma((C // 2,)), dma((C // 2,)),
            dma((C,)), dma((C,)), dma((C,)), dma((C,)),
            dma, dma,
            dma((C // 2,)), dma((C // 2,)),
            dma, dma,
        ],
        compiler_params=pltpu.CompilerParams(
            collective_id=0, has_side_effects=True, vmem_limit_bytes=60 * 1024 * 1024
        ),
    )(
        emb_values, emb_scales.T, coarse_ids, centroids, codes_one, codes_two,
        jnp.swapaxes(codebook_init, 1, 2),
    )
    gap, book_one, book_two, distortion = pl.pallas_call(
        write_out,
        out_shape=tuple(jax.ShapeDtypeStruct(a.shape, a.dtype) for a in results),
        in_specs=[vmem] * 4,
        out_specs=(vmem,) * 4,
        compiler_params=pltpu.CompilerParams(vmem_limit_bytes=60 * 1024 * 1024),
    )(*results)
    return gap.reshape(N), jnp.swapaxes(book_one, 1, 2), jnp.swapaxes(book_two, 1, 2), distortion


def solution(mesh):
    placed = (
        P(("cent", "rows"), None),
        P(("cent", "rows"), None),
        P(None, "rows"),
        P("cent", None),
        P("rows", "cent"),
        P("rows", "cent"),
        P("rows", None, None),
    )
    return jax.shard_map(
        functools.partial(on_device, mesh.shape["cent"], mesh.shape["rows"]),
        mesh=mesh,
        in_specs=placed,
        out_specs=(
            P(("cent", "rows")),
            P("rows", None, None),
            P("rows", None, None),
            P("rows", "cent"),
        ),
        check_vma=False,
    )
```
